32 devices in a mesh: label: 4 (over y, x), batch: 8 (over z, core).
Axes of the slice: x: 2, y: 2, z: 4, core: 2. Of those that a mesh axis runs over, the one named last changes fastest.
Arguments:
- queries: bfloat16 [4096, 768], P('batch'), may hold values from -6 to 6
- slab: bfloat16 [51200, 768], P(('label', 'batch')), may hold values from -0.21875 to 0.21875
- positives: int32 [4096, 51200], P('batch', 'label'), may hold values 0 or 1
Outputs:
- query_grad: bfloat16 [4096, 768], P('batch')
- slab_grad: bfloat16 [51200, 768], P(('label', 'batch'))
The draws below stay inside these ranges and needn't reach their ends.
All inputs are finite; a program needn't handle non-finite values. No bound on the sum of `positives` on one device may be relied on, other than what follows from the above.
Results may differ from the reference program's by a relative error of at most 0.0037.
Values may be sent and summed in bfloat16 or wider, within the bound.
A program may use at most 192 MiB of HBM per device.

```python
import jax
import jax.numpy as jnp
from jax import lax

D = 768
LABELS = 51200
QUERIES = 4096


def plant(array, key, smallest, high):
    shape = array.shape
    spot = [jax.random.randint(jax.random.fold_in(key, axis), (), 0, shape[axis]) for axis in range(len(shape))]
    array = array.at[tuple(spot)].set(smallest)
    longest = shape.index(max(shape))
    spot[longest] = (spot[longest] + 1) % shape[longest]
    return array.at[tuple(spot)].set(high)


def steps_of(key, shape, cuts, low, high):
    level, own = 1.0, jax.random.fold_in(key, 6)
    for dim, shards_of in cuts:
        steps = jnp.exp(jax.random.uniform(jax.random.fold_in(own, dim), (shards_of,), jnp.float32, low / len(cuts), high / len(cuts)))
        level = level * jnp.repeat(steps, shape[dim] // shards_of).reshape([-1 if axis == dim else 1 for axis in range(len(shape))])
    return level


def noise(key, shape, scale, limit, split=(), dtype=jnp.bfloat16):
    entries = scale * jax.random.normal(key, shape, jnp.float32)
    if split:
        entries = entries * steps_of(key, shape, split, -0.22, 0.18)
    return jnp.clip(entries, -limit, limit).astype(dtype)


def setup_inputs(seed: int = 0) -> dict:
    key_of = jax.random.split(jax.random.key(seed), 4)
    queries = noise(key_of[0], (QUERIES, D), 1.0, 6.0, ((0, 8),))
    slab = noise(key_of[1], (LABELS, D), D ** -0.5, 0.21875, ((0, 32),))
    positives = plant((jax.random.randint(key_of[2], (QUERIES, LABELS), 0, 4) < 1).astype(jnp.int32), jax.random.fold_in(key_of[2], 1), 0, 1)
    return {"queries": queries, "slab": slab, "positives": positives}


loss_weight = 0.0625


def reference(queries, slab, positives):
    blocks = 16
    width = LABELS // blocks
    slab_blocks = slab.reshape(blocks, width, D)
    mask_blocks = positives.reshape(QUERIES, blocks, width).transpose(1, 0, 2)

    def step(carry, pair):
        weights, labels = pair
        logits = lax.dot_general(queries, weights, (((1,), (1,)), ((), ())), preferred_element_type=jnp.float32)
        grad = ((jax.nn.sigmoid(logits) - labels.astype(jnp.float32)) * loss_weight).astype(jnp.bfloat16)
        carry = carry + jnp.dot(grad, weights, preferred_element_type=jnp.float32)
        slab_part = lax.dot_general(grad, queries, (((0,), (0,)), ((), ())), preferred_element_type=jnp.float32)
        return carry, slab_part.astype(jnp.bfloat16)

    start = jnp.zeros((QUERIES, D), jnp.float32)
    total, parts = lax.scan(step, start, (slab_blocks, mask_blocks))
    return total.astype(jnp.bfloat16), parts.reshape(LABELS, D)
```

```python
import jax
import jax.numpy as jnp
from jax import lax
from jax.experimental import pallas as pl
from jax.experimental.pallas import tpu as pltpu
from jax.sharding import PartitionSpec as P

loss_weight = 0.0625
MESH = pl.DeviceIdType.MESH
F32, BF16 = jnp.float32, jnp.bfloat16
PARTS = 5
NEAR, MID = 4, 7


def plain(queries, slab, positives):
    piece = lax.all_gather(slab, "batch", axis=0, tiled=True)
    logits = lax.dot_general(queries, piece, (((1,), (1,)), ((), ())), preferred_element_type=F32)
    grad = ((jax.nn.sigmoid(logits) - positives.astype(F32)) * loss_weight).astype(BF16)
    query_grad = lax.psum(jnp.dot(grad, piece, preferred_element_type=F32), "label").astype(BF16)
    slab_grad = lax.psum_scatter(
        lax.dot_general(grad, queries, (((0,), (0,)), ((), ())), preferred_element_type=F32),
        "batch",
        scatter_dimension=0,
        tiled=True,
    ).astype(BF16)
    return query_grad, slab_grad


def remote(src, dst, send, recv, device):
    return pltpu.make_async_remote_copy(
        src_ref=src, dst_ref=dst, send_sem=send, recv_sem=recv, device_id=device, device_id_type=MESH
    )


def line_kernel(
    n, win,
    q_ref, slab_ref, pos_ref,
    qout, sout, posin,
    G, RS, PS, qb, qacc, pt, gs, qr, xr,
    loc_sem, q_send, q_recv, p_send, p_recv, pt_sem, g_send, g_recv, r_send, r_recv, a_send, a_recv, x_send, x_recv,
):
    K, w, D = slab_ref.shape
    H = 2 * K
    rows = q_ref.shape[0]
    half = rows // 2
    l = lax.axis_index("label")
    b = lax.axis_index("batch")
    z, c = b // 2, b % 2
    zm = n - 1 - z
    sib = {"batch": b + 1 - 2 * c}
    right, left = {"batch": b + 2}, {"batch": b - 2}
    partner = ({"label": l + 1 - 2 * (l % 2)}, {"label": l + 2 - 4 * (l // 2)})
    has_r, has_l = z < n - 1, z > 0

    barrier = pltpu.get_barrier_semaphore()
    for dev in (sib, *partner):
        pl.semaphore_signal(barrier, inc=1, device_id=dev, device_id_type=MESH)

    @pl.when(has_r)
    def _():
        pl.semaphore_signal(barrier, inc=1, device_id=right, device_id_type=MESH)

    @pl.when(has_l)
    def _():
        pl.semaphore_signal(barrier, inc=1, device_id=left, device_id_type=MESH)

    def local_slab(k):
        return pltpu.make_async_copy(slab_ref.at[k], G.at[z, k], loc_sem.at[k])

    q_own = pltpu.make_async_copy(q_ref, qb.at[0], loc_sem.at[K])
    q_own.start()

    @pl.loop(0, K)
    def _(k):
        local_slab(k).start()

    qacc[...] = jnp.zeros_like(qacc)
    pl.semaphore_wait(barrier, 3 + has_r.astype(jnp.int32) + has_l.astype(jnp.int32))

    def column(block, core, k):
        return pl.multiple_of(block * (2 * K * w) + core * (K * w) + k * w - 64 * ((k + core) % 2), 128)

    def own_right(k):
        return remote(slab_ref.at[k], G.at[z, k], g_send.at[0, z, k], g_recv.at[z, k], right)

    def own_left(k):
        return remote(slab_ref.at[k], G.at[z, k], g_send.at[1, z, k], g_recv.at[z, k], left)

    def pass_right(block, k):
        return remote(G.at[block, k], G.at[block, k], g_send.at[0, block, k], g_recv.at[block, k], right)

    def pass_left(block, k):
        return remote(G.at[block, k], G.at[block, k], g_send.at[1, block, k], g_recv.at[block, k], left)

    def swap(block, k):
        return remote(
            pos_ref.at[:, pl.ds(column(block, 1 - c, k), win)], posin.at[block, k],
            p_send.at[block, k], p_recv.at[block, k], sib,
        )

    def send_q():
        return remote(q_ref, qb.at[1], q_send, q_recv, sib)

    def sum_right(dest, h):
        return remote(RS.at[dest, h], RS.at[dest, h], r_send.at[dest, h], r_recv.at[dest, h], right)

    def sum_left(dest, h):
        slot = jnp.where(dest == z - 1, n, dest)
        return remote(RS.at[dest, h], RS.at[slot, h], r_send.at[dest, h], r_recv.at[slot, h], left)

    def arrived(slot, h):
        remote(RS.at[slot, h], RS.at[slot, h], r_send.at[0, 0], r_recv.at[slot, h], sib).wait_recv()

    @pl.loop(0, K)
    def _(k):
        @pl.when(has_r)
        def _():
            own_right(k).start()

        @pl.when(has_l)
        def _():
            own_left(k).start()

        @pl.when(k == 0)
        def _():
            send_q().start()

        swap(z, k).start()

    @pl.loop(0, (n - 1) * K)
    def _(j):
        d, k = j // K + 1, j % K

        @pl.when(z + d < n)
        def _():
            swap(z + d, k).start()

        @pl.when(z - d >= 0)
        def _():
            swap(z - d, k).start()

    q_own.wait()
    send_q().wait_recv()

    def marks_of(block, k):
        mine = pltpu.make_async_copy(pos_ref.at[:, pl.ds(column(block, c, k), win)], pt.at[0], pt_sem.at[0])
        theirs = pltpu.make_async_copy(posin.at[block, k], pt.at[1], pt_sem.at[1])
        return mine, theirs

    def fetch(block, k):
        mine, theirs = marks_of(block, k)
        mine.start()
        swap(block, k).wait_recv()
        theirs.start()

    def tile(block, k):
        for copy in marks_of(block, k):
            copy.wait()
        odd = (k + c) % 2 == 1

        @pl.loop(0, 2)
        def _(h):
            labels = G[block, k]
            logits = lax.dot_general(qb[h], labels, (((1,), (1,)), ((), ())), preferred_element_type=F32)
            marks = jnp.where(odd, pt[h, :, 64 : 64 + w], pt[h, :, 0:w]).astype(F32)
            grad = ((jax.nn.sigmoid(logits) - marks) * loss_weight).astype(BF16)
            gs[h] = grad
            qacc[h] += jnp.dot(grad, labels, preferred_element_type=F32)

        grads = gs[...].reshape(2 * rows, w)
        both = qb[...].reshape(2 * rows, D)
        part = lax.dot_general(grads, both, (((0,), (0,)), ((), ())), preferred_element_type=F32)
        PS[block, pl.ds(2 * k, 2)] = part.reshape(2, w // 2, D)

    def turn(i, at):
        near_far = jnp.where(i < H, 1, jnp.where(i < 2 * H, 2, jnp.where(i < 3 * H, 3, 1)))
        near_h = i - jnp.where(i < H, H - NEAR, jnp.where(i < 2 * H, H, jnp.where(i < 3 * H, 2 * H, 3 * H - NEAR)))
        near_ok = (i >= H - NEAR) & (i < 4 * H - NEAR)
        m = i - NEAR
        mid_far = jnp.where((m >= 2 * H) & (m < 3 * H), 3, 2)
        mid_h = m - jnp.where(m < 2 * H, H, jnp.where(m < 3 * H, 2 * H, 3 * H - MID))
        mid_ok = (m >= H) & ((m < H + MID) | (m >= 2 * H)) & (m < 4 * H - MID)
        last_h = i - 2 * H - MID
        last_ok = (last_h >= 0) & (last_h < H)
        far = jnp.where(at == 0, near_far, jnp.where(at == 1, mid_far, 3))
        h = jnp.where(at == 0, near_h, jnp.where(at == 1, mid_h, last_h))
        ok = ((at == 0) & near_ok) | ((at == 1) & mid_ok) | ((at == 2) & last_ok)
        return far, h, ok

    def sums(i):
        for at, going_right in ((z, True), (zm, False)):
            far, h, ok = turn(i, at)
            dest = far if going_right else n - 1 - far

            @pl.when(ok)
            def _(at=at, h=h, dest=dest, going_right=going_right):
                @pl.when(at > 0)
                def _():
                    arrived(dest, h)
                    RS[dest, h] = (RS[dest, h].astype(F32) + PS[dest, h]).astype(BF16)

                @pl.when(at == 0)
                def _():
                    RS[dest, h] = PS[dest, h].astype(BF16)

                (sum_right if going_right else sum_left)(dest, h).start()

        t = i - 3 * H

        @pl.when((t >= 0) & (t < H))
        def _():
            @pl.when(has_l)
            def _():
                arrived(z, t)
                PS[z, t] += RS[z, t].astype(F32)

            @pl.when(has_r)
            def _():
                arrived(n, t)
                PS[z, t] += RS[n, t].astype(F32)

            sout[t] = PS[z, t].astype(BF16)

    @pl.loop(0, (n - 1) * K)
    def _(j):
        d, k = j // K + 1, j % K

        @pl.when(j < K)
        def _():
            local_slab(k).wait()

        @pl.loop(0, 3)
        def _(s):
            block = jnp.where(s == 0, z, jnp.where(s == 1, z + d, z - d))
            busy = ((s == 0) & (j < K)) | ((s > 0) & (block >= 0) & (block < n))

            @pl.when(busy)
            def _():
                fetch(block, k)

            @pl.when((s == 1) & (block < n))
            def _():
                pass_left(block, k).wait_recv()

                @pl.when(has_l)
                def _():
                    pass_left(block, k).start()

            @pl.when((s == 2) & (block >= 0))
            def _():
                pass_right(block, k).wait_recv()

                @pl.when(has_r)
                def _():
                    pass_right(block, k).start()

            @pl.when(busy)
            def _():
                tile(block, k)

        @pl.loop(2 * j, 2 * j + 2)
        def _(i):
            sums(i)

    theirs = remote(qacc.at[1], qr, a_send, a_recv, sib)

    def over(stage, h):
        src = qacc.at[0, pl.ds(h * half, half)] if stage == 0 else xr.at[0, h]
        dev = partner[h] if stage == 0 else partner[1 - h]
        return remote(src, xr.at[stage, h], x_send.at[stage, h], x_recv.at[stage, h], dev)

    theirs.start()
    pl.loop(3 * H, 3 * H + 1)(sums)
    theirs.wait_recv()
    qacc[0] += qr[...]
    for h in range(2):
        over(0, h).start()
    pl.loop(3 * H + 1, 3 * H + H // 2)(sums)
    for h in range(2):
        over(0, h).wait_recv()
        xr[0, h] += qacc[0, h * half : (h + 1) * half, :]
        over(1, h).start()
    pl.loop(3 * H + H // 2, 4 * H - 1)(sums)
    for h in range(2):
        over(1, h).wait_recv()
        qout[h * half : (h + 1) * half, :] = (xr[0, h] + xr[1, h]).astype(BF16)
    pl.loop(4 * H - 1, 4 * H)(sums)

    for h in range(2):
        over(0, h).wait_send()
        over(1, h).wait_send()
    theirs.wait_send()
    send_q().wait_send()

    @pl.loop(0, n * K)
    def _(j):
        block, k = j // K, j % K
        swap(block, k).wait_send()

        @pl.when(has_r & (block <= z))
        def _():
            pass_right(block, k).wait_send()

        @pl.when(has_l & (block >= z))
        def _():
            pass_left(block, k).wait_send()

        @pl.when(block != z)
        def _():
            sum_right(block, 2 * k).wait_send()
            sum_right(block, 2 * k + 1).wait_send()


def copy_kernel(q_ref, s_ref, q_out, s_out, q_vmem, s_vmem, sem):
    K, rows = s_ref.shape[0], q_ref.shape[0] // 2
    parts = [(s_ref.at[k], s_vmem.at[k], s_out.at[k]) for k in range(K)]
    for h in range(2):
        part = pl.ds(h * rows, rows)
        parts.append((q_ref.at[part], q_vmem.at[part], q_out.at[part]))
    come = [pltpu.make_async_copy(src, mid, sem.at[0, i]) for i, (src, mid, _) in enumerate(parts)]
    go = [pltpu.make_async_copy(mid, dst, sem.at[1, i]) for i, (_, mid, dst) in enumerate(parts)]
    for copy in come:
        copy.start()
    for before, after in zip(come, go):
        before.wait()
        after.start()
    for copy in go:
        copy.wait()


def hand_over(query_grad, slab_grad):
    hbm = pl.BlockSpec(memory_space=pl.ANY)
    return pl.pallas_call(
        copy_kernel,
        out_shape=tuple(jax.ShapeDtypeStruct(x.shape, x.dtype) for x in (query_grad, slab_grad)),
        in_specs=[hbm, hbm],
        out_specs=(hbm, hbm),
        scratch_shapes=[
            pltpu.VMEM(query_grad.shape, query_grad.dtype),
            pltpu.VMEM(slab_grad.shape, slab_grad.dtype),
            pltpu.SemaphoreType.DMA((2, slab_grad.shape[0] + 2)),
        ],
    )(query_grad, slab_grad)


def fused(n, queries, slab, positives):
    rows, D = queries.shape
    R = slab.shape[0]
    K, w = PARTS, R // PARTS
    win = w + 64
    vmem = pl.BlockSpec(memory_space=pltpu.VMEM)
    hbm = pl.BlockSpec(memory_space=pl.ANY)
    dma = pltpu.SemaphoreType.DMA
    query_grad, slab_grad, _ = pl.pallas_call(
        lambda *refs: line_kernel(n, win, *refs),
        out_shape=(
            jax.ShapeDtypeStruct((rows, D), BF16),
            jax.ShapeDtypeStruct((2 * K, w // 2, D), BF16),
            jax.ShapeDtypeStruct((n, K, rows, win), jnp.int32),
        ),
        in_specs=[hbm, hbm, hbm],
        out_specs=(vmem, vmem, hbm),
        scratch_shapes=[
            pltpu.VMEM((n, K, w, D), BF16),
            pltpu.VMEM((n + 1, 2 * K, w // 2, D), BF16),
            pltpu.VMEM((n, 2 * K, w // 2, D), F32),
            pltpu.VMEM((2, rows, D), BF16),
            pltpu.VMEM((2, rows, D), F32),
            pltpu.VMEM((2, rows, win), jnp.int32),
            pltpu.VMEM((2, rows, w), BF16),
            pltpu.VMEM((rows, D), F32),
            pltpu.VMEM((2, 2, rows // 2, D), F32),
            dma((K + 1,)), dma, dma, dma((n, K)), dma((n, K)), dma((2,)),
            dma((2, n, K)), dma((n, K)), dma((n, 2 * K)), dma((n + 1, 2 * K)), dma, dma, dma((2, 2)), dma((2, 2)),
        ],
        compiler_params=pltpu.CompilerParams(
            collective_id=0, has_side_effects=True, vmem_limit_bytes=62 * 2**20
        ),
        cost_estimate=pl.CostEstimate(
            flops=12 * rows * n * R * D, bytes_accessed=rows * n * R * 8, transcendentals=2 * rows * n * R
        ),
    )(queries, slab.reshape(K, w, D), positives)
    query_grad, slab_grad = hand_over(query_grad, slab_grad)
    return query_grad, slab_grad.reshape(R, D)


def solution(mesh):
    labels, batch = mesh.shape["label"], mesh.shape["batch"]

    def per_device(queries, slab, positives):
        R = slab.shape[0]
        fits = labels == 4 and batch == 8 and R % (PARTS * 64) == 0 and (R // PARTS) % 128 == 64
        if fits and (R // 64) % 2 == 1 and queries.shape[0] % 32 == 0 and R <= 1600:
            return fused(batch // 2, queries, slab, positives)
        return plain(queries, slab, positives)

    return jax.shard_map(
        per_device,
        mesh=mesh,
        in_specs=(P("batch", None), P(("label", "batch"), None), P("batch", "label")),
        out_specs=(P("batch", None), P(("label", "batch"), None)),
        check_vma=False,
    )
```

```python
import jax
import jax.numpy as jnp
from jax import lax
from jax.experimental import pallas as pl
from jax.experimental.pallas import tpu as pltpu
from jax.sharding import PartitionSpec as P

loss_weight = 0.0625
MESH = pl.DeviceIdType.MESH
F32, BF16 = jnp.float32, jnp.bfloat16
PARTS = 5
NEAR, MID = 4, 7


def plain(queries, slab, positives):
    piece = lax.all_gather(slab, "batch", axis=0, tiled=True)
    logits = lax.dot_general(queries, piece, (((1,), (1,)), ((), ())), preferred_element_type=F32)
    grad = ((jax.nn.sigmoid(logits) - positives.astype(F32)) * loss_weight).astype(BF16)
    query_grad = lax.psum(jnp.dot(grad, piece, preferred_element_type=F32), "label").astype(BF16)
    slab_grad = lax.psum_scatter(
        lax.dot_general(grad, queries, (((0,), (0,)), ((), ())), preferred_element_type=F32),
        "batch",
        scatter_dimension=0,
        tiled=True,
    ).astype(BF16)
    return query_grad, slab_grad


def remote(src, dst, send, recv, device):
    return pltpu.make_async_remote_copy(
        src_ref=src, dst_ref=dst, send_sem=send, recv_sem=recv, device_id=device, device_id_type=MESH
    )


def line_kernel(
    n, win,
    q_ref, slab_ref, pos_ref,
    qout, sout, posin,
    G, RS, PS, qb, qacc, pt, gs, qr, xr,
    loc_sem, q_send, q_recv, p_send, p_recv, pt_sem, g_send, g_recv, r_send, r_recv, a_send, a_recv, x_send, x_recv,
):
    K, w, D = slab_ref.shape
    H = 2 * K
    rows = q_ref.shape[0]
    half = rows // 2
    l = lax.axis_index("label")
    b = lax.axis_index("batch")
    z, c = b // 2, b % 2
    zm = n - 1 - z
    sib = {"batch": b + 1 - 2 * c}
    right, left = {"batch": b + 2}, {"batch": b - 2}
    partner = ({"label": l + 1 - 2 * (l % 2)}, {"label": l + 2 - 4 * (l // 2)})
    has_r, has_l = z < n - 1, z > 0

    barrier = pltpu.get_barrier_semaphore()
    for dev in (sib, *partner):
        pl.semaphore_signal(barrier, inc=1, device_id=dev, device_id_type=MESH)

    @pl.when(has_r)
    def _():
        pl.semaphore_signal(barrier, inc=1, device_id=right, device_id_type=MESH)

    @pl.when(has_l)
    def _():
        pl.semaphore_signal(barrier, inc=1, device_id=left, device_id_type=MESH)

    def local_slab(k):
        return pltpu.make_async_copy(slab_ref.at[k], G.at[z, k], loc_sem.at[k])

    q_own = pltpu.make_async_copy(q_ref, qb.at[0], loc_sem.at[K])
    q_own.start()

    @pl.loop(0, K)
    def _(k):
        local_slab(k).start()

    qacc[...] = jnp.zeros_like(qacc)
    pl.semaphore_wait(barrier, 3 + has_r.astype(jnp.int32) + has_l.astype(jnp.int32))

    def column(block, core, k):
        return pl.multiple_of(block * (2 * K * w) + core * (K * w) + k * w - 64 * ((k + core) % 2), 128)

    def own_right(k):
        return remote(slab_ref.at[k], G.at[z, k], g_send.at[0, z, k], g_recv.at[z, k], right)

    def own_left(k):
        return remote(slab_ref.at[k], G.at[z, k], g_send.at[1, z, k], g_recv.at[z, k], left)

    def pass_right(block, k):
        return remote(G.at[block, k], G.at[block, k], g_send.at[0, block, k], g_recv.at[block, k], right)

    def pass_left(block, k):
        return remote(G.at[block, k], G.at[block, k], g_send.at[1, block, k], g_recv.at[block, k], left)

    def swap(block, k):
        return remote(
            pos_ref.at[:, pl.ds(column(block, 1 - c, k), win)], posin.at[block, k],
            p_send.at[block, k], p_recv.at[block, k], sib,
        )

    def send_q():
        return remote(q_ref, qb.at[1], q_send, q_recv, sib)

    def sum_right(dest, h):
        return remote(RS.at[dest, h], RS.at[dest, h], r_send.at[dest, h], r_recv.at[dest, h], right)

    def sum_left(dest, h):
        slot = jnp.where(dest == z - 1, n, dest)
        return remote(RS.at[dest, h], RS.at[slot, h], r_send.at[dest, h], r_recv.at[slot, h], left)

    def arrived(slot, h):
        remote(RS.at[slot, h], RS.at[slot, h], r_send.at[0, 0], r_recv.at[slot, h], sib).wait_recv()

    @pl.loop(0, K)
    def _(k):
        @pl.when(has_r)
        def _():
            own_right(k).start()

        @pl.when(has_l)
        def _():
            own_left(k).start()

        @pl.when(k == 0)
        def _():
            send_q().start()

        swap(z, k).start()

    @pl.loop(0, (n - 1) * K)
    def _(j):
        d, k = j // K + 1, j % K

        @pl.when(z + d < n)
        def _():
            swap(z + d, k).start()

        @pl.when(z - d >= 0)
        def _():
            swap(z - d, k).start()

    q_own.wait()
    send_q().wait_recv()

    def marks_of(block, k):
        mine = pltpu.make_async_copy(pos_ref.at[:, pl.ds(column(block, c, k), win)], pt.at[0], pt_sem.at[0])
        theirs = pltpu.make_async_copy(posin.at[block, k], pt.at[1], pt_sem.at[1])
        return mine, theirs

    def fetch(block, k):
        mine, theirs = marks_of(block, k)
        mine.start()
        swap(block, k).wait_recv()
        theirs.start()

    def tile(block, k):
        for copy in marks_of(block, k):
            copy.wait()
        odd = (k + c) % 2 == 1

        @pl.loop(0, 2)
        def _(h):
            labels = G[block, k]
            logits = lax.dot_general(qb[h], labels, (((1,), (1,)), ((), ())), preferred_element_type=F32)
            marks = jnp.where(odd, pt[h, :, 64 : 64 + w], pt[h, :, 0:w]).astype(F32)
            grad = ((jax.nn.sigmoid(logits) - marks) * loss_weight).astype(BF16)
            gs[h] = grad
            qacc[h] += jnp.dot(grad, labels, preferred_element_type=F32)

        grads = gs[...].reshape(2 * rows, w)
        both = qb[...].reshape(2 * rows, D)
        part = lax.dot_general(grads, both, (((0,), (0,)), ((), ())), preferred_element_type=F32)
        PS[block, pl.ds(2 * k, 2)] = part.reshape(2, w // 2, D)

    def turn(i, at):
        near_far = jnp.where(i < H, 1, jnp.where(i < 2 * H, 2, jnp.where(i < 3 * H, 3, 1)))
        near_h = i - jnp.where(i < H, H - NEAR, jnp.where(i < 2 * H, H, jnp.where(i < 3 * H, 2 * H, 3 * H - NEAR)))
        near_ok = (i >= H - NEAR) & (i < 4 * H - NEAR)
        m = i - NEAR
        mid_far = jnp.where((m >= 2 * H) & (m < 3 * H), 3, 2)
        mid_h = m - jnp.where(m < 2 * H, H, jnp.where(m < 3 * H, 2 * H, 3 * H - MID))
        mid_ok = (m >= H) & ((m < H + MID) | (m >= 2 * H)) & (m < 4 * H - MID)
        last_h = i - 2 * H - MID
        last_ok = (last_h >= 0) & (last_h < H)
        far = jnp.where(at == 0, near_far, jnp.where(at == 1, mid_far, 3))
        h = jnp.where(at == 0, near_h, jnp.where(at == 1, mid_h, last_h))
        ok = ((at == 0) & near_ok) | ((at == 1) & mid_ok) | ((at == 2) & last_ok)
        return far, h, ok

    def sums(i):
        for at, going_right in ((z, True), (zm, False)):
            far, h, ok = turn(i, at)
            dest = far if going_right else n - 1 - far

            @pl.when(ok)
            def _(at=at, h=h, dest=dest, going_right=going_right):
                @pl.when(at > 0)
                def _():
                    arrived(dest, h)
                    RS[dest, h] = (RS[dest, h].astype(F32) + PS[dest, h]).astype(BF16)

                @pl.when(at == 0)
                def _():
                    RS[dest, h] = PS[dest, h].astype(BF16)

                (sum_right if going_right else sum_left)(dest, h).start()

        t = i - 3 * H

        @pl.when((t >= 0) & (t < H))
        def _():
            @pl.when(has_l)
            def _():
                arrived(z, t)
                PS[z, t] += RS[z, t].astype(F32)

            @pl.when(has_r)
            def _():
                arrived(n, t)
                PS[z, t] += RS[n, t].astype(F32)

            sout[t] = PS[z, t].astype(BF16)

    @pl.loop(0, (n - 1) * K)
    def _(j):
        d, k = j // K + 1, j % K

        @pl.when(j < K)
        def _():
            local_slab(k).wait()

        @pl.loop(0, 3)
        def _(s):
            block = jnp.where(s == 0, z, jnp.where(s == 1, z + d, z - d))
            busy = ((s == 0) & (j < K)) | ((s > 0) & (block >= 0) & (block < n))

            @pl.when(busy)
            def _():
                fetch(block, k)

            @pl.when((s == 1) & (block < n))
            def _():
                pass_left(block, k).wait_recv()

                @pl.when(has_l)
                def _():
                    pass_left(block, k).start()

            @pl.when((s == 2) & (block >= 0))
            def _():
                pass_right(block, k).wait_recv()

                @pl.when(has_r)
                def _():
                    pass_right(block, k).start()

            @pl.when(busy)
            def _():
                tile(block, k)

        @pl.loop(2 * j, 2 * j + 2)
        def _(i):
            sums(i)

    theirs = remote(qacc.at[1], qr, a_send, a_recv, sib)

    def over(stage, h):
        src = qacc.at[0, pl.ds(h * half, half)] if stage == 0 else xr.at[0, h]
        dev = partner[h] if stage == 0 else partner[1 - h]
        return remote(src, xr.at[stage, h], x_send.at[stage, h], x_recv.at[stage, h], dev)

    theirs.start()
    pl.loop(3 * H, 3 * H + 1)(sums)
    theirs.wait_recv()
    qacc[0] += qr[...]
    for h in range(2):
        over(0, h).start()
    pl.loop(3 * H + 1, 3 * H + H // 2)(sums)
    for h in range(2):
        over(0, h).wait_recv()
        xr[0, h] += qacc[0, h * half : (h + 1) * half, :]
        over(1, h).start()
    pl.loop(3 * H + H // 2, 4 * H - 1)(sums)
    for h in range(2):
        over(1, h).wait_recv()
        qout[h * half : (h + 1) * half, :] = (xr[0, h] + xr[1, h]).astype(BF16)
    pl.loop(4 * H - 1, 4 * H)(sums)

    for h in range(2):
        over(0, h).wait_send()
        over(1, h).wait_send()
    theirs.wait_send()
    send_q().wait_send()

    @pl.loop(0, n * K)
    def _(j):
        block, k = j // K, j % K
        swap(block, k).wait_send()

        @pl.when(has_r & (block <= z))
        def _():
            pass_right(block, k).wait_send()

        @pl.when(has_l & (block >= z))
        def _():
            pass_left(block, k).wait_send()

        @pl.when(block != z)
        def _():
            sum_right(block, 2 * k).wait_send()
            sum_right(block, 2 * k + 1).wait_send()


def copy_kernel(q_ref, s_ref, q_out, s_out, sem):
    copies = [pltpu.make_async_copy(q_ref, q_out, sem.at[0]), pltpu.make_async_copy(s_ref, s_out, sem.at[1])]
    for copy in copies:
        copy.start()
    for copy in copies:
        copy.wait()


def hand_over(query_grad, slab_grad):
    vmem = pl.BlockSpec(memory_space=pltpu.VMEM)
    hbm = pl.BlockSpec(memory_space=pl.ANY)
    return pl.pallas_call(
        copy_kernel,
        out_shape=tuple(jax.ShapeDtypeStruct(x.shape, x.dtype) for x in (query_grad, slab_grad)),
        in_specs=[vmem, vmem],
        compiler_params=pltpu.CompilerParams(vmem_limit_bytes=2**20),
        out_specs=(hbm, hbm),
        scratch_shapes=[pltpu.SemaphoreType.DMA((2,))],
    )(*(pltpu.with_memory_space_constraint(x, pltpu.VMEM) for x in (query_grad, slab_grad)))


def fused(n, queries, slab, positives):
    rows, D = queries.shape
    R = slab.shape[0]
    K, w = PARTS, R // PARTS
    win = w + 64
    vmem = pl.BlockSpec(memory_space=pltpu.VMEM)
    hbm = pl.BlockSpec(memory_space=pl.ANY)
    dma = pltpu.SemaphoreType.DMA
    query_grad, slab_grad, _ = pl.pallas_call(
        lambda *refs: line_kernel(n, win, *refs),
        out_shape=(
            pltpu.VMEM((rows, D), BF16),
            pltpu.VMEM((2 * K, w // 2, D), BF16),
            jax.ShapeDtypeStruct((n, K, rows, win), jnp.int32),
        ),
        in_specs=[hbm, hbm, hbm],
        out_specs=(vmem, vmem, hbm),
        scratch_shapes=[
            pltpu.VMEM((n, K, w, D), BF16),
            pltpu.VMEM((n + 1, 2 * K, w // 2, D), BF16),
            pltpu.VMEM((n, 2 * K, w // 2, D), F32),
            pltpu.VMEM((2, rows, D), BF16),
            pltpu.VMEM((2, rows, D), F32),
            pltpu.VMEM((2, rows, win), jnp.int32),
            pltpu.VMEM((2, rows, w), BF16),
            pltpu.VMEM((rows, D), F32),
            pltpu.VMEM((2, 2, rows // 2, D), F32),
            dma((K + 1,)), dma, dma, dma((n, K)), dma((n, K)), dma((2,)),
            dma((2, n, K)), dma((n, K)), dma((n, 2 * K)), dma((n + 1, 2 * K)), dma, dma, dma((2, 2)), dma((2, 2)),
        ],
        compiler_params=pltpu.CompilerParams(
            collective_id=0, has_side_effects=True, vmem_limit_bytes=58 * 2**20
        ),
        cost_estimate=pl.CostEstimate(
            flops=12 * rows * n * R * D, bytes_accessed=rows * n * R * 8, transcendentals=2 * rows * n * R
        ),
    )(queries, slab.reshape(K, w, D), positives)
    query_grad, slab_grad = hand_over(query_grad, slab_grad)
    return query_grad, slab_grad.reshape(R, D)


def solution(mesh):
    labels, batch = mesh.shape["label"], mesh.shape["batch"]

    def per_device(queries, slab, positives):
        R = slab.shape[0]
        fits = labels == 4 and batch == 8 and R % (PARTS * 64) == 0 and (R // PARTS) % 128 == 64
        if fits and (R // 64) % 2 == 1 and queries.shape[0] % 32 == 0 and R <= 1600:
            return fused(batch // 2, queries, slab, positives)
        return plain(queries, slab, positives)

    return jax.shard_map(
        per_device,
        mesh=mesh,
        in_specs=(P("batch", None), P(("label", "batch"), None), P("batch", "label")),
        out_specs=(P("batch", None), P(("label", "batch"), None)),
        check_vma=False,
    )
```

```python
import jax
import jax.numpy as jnp
from jax import lax
from jax.experimental import pallas as pl
from jax.experimental.pallas import tpu as pltpu
from jax.sharding import PartitionSpec as P

loss_weight = 0.0625
MESH = pl.DeviceIdType.MESH
F32, BF16 = jnp.float32, jnp.bfloat16
PARTS = 5
NEAR, MID, LAG = 2, 3, 5


def plain(queries, slab, positives):
    piece = lax.all_gather(slab, "batch", axis=0, tiled=True)
    logits = lax.dot_general(queries, piece, (((1,), (1,)), ((), ())), preferred_element_type=F32)
    grad = ((jax.nn.sigmoid(logits) - positives.astype(F32)) * loss_weight).astype(BF16)
    query_grad = lax.psum(jnp.dot(grad, piece, preferred_element_type=F32), "label").astype(BF16)
    slab_grad = lax.psum_scatter(
        lax.dot_general(grad, queries, (((0,), (0,)), ((), ())), preferred_element_type=F32),
        "batch",
        scatter_dimension=0,
        tiled=True,
    ).astype(BF16)
    return query_grad, slab_grad


def remote(src, dst, send, recv, device):
    return pltpu.make_async_remote_copy(
        src_ref=src, dst_ref=dst, send_sem=send, recv_sem=recv, device_id=device, device_id_type=MESH
    )


def line_kernel(
    n, win,
    q_ref, slab_ref, pos_ref,
    qout, sout, posin,
    G, RS, PS, qb, qacc, pt, gs, qr, xr,
    loc_sem, q_send, q_recv, p_send, p_recv, pt_sem, g_send, g_recv, r_send, r_recv, a_send, a_recv, x_send, x_recv,
):
    K, w, D = slab_ref.shape
    H = K
    rows = q_ref.shape[0]
    half = rows // 2
    l = lax.axis_index("label")
    b = lax.axis_index("batch")
    z, c = b // 2, b % 2
    zm = n - 1 - z
    sib = {"batch": b + 1 - 2 * c}
    right, left = {"batch": b + 2}, {"batch": b - 2}
    partner = ({"label": l + 1 - 2 * (l % 2)}, {"label": l + 2 - 4 * (l // 2)})
    has_r, has_l = z < n - 1, z > 0

    barrier = pltpu.get_barrier_semaphore()
    for dev in (sib, *partner):
        pl.semaphore_signal(barrier, inc=1, device_id=dev, device_id_type=MESH)

    @pl.when(has_r)
    def _():
        pl.semaphore_signal(barrier, inc=1, device_id=right, device_id_type=MESH)

    @pl.when(has_l)
    def _():
        pl.semaphore_signal(barrier, inc=1, device_id=left, device_id_type=MESH)

    def local_slab(k):
        return pltpu.make_async_copy(slab_ref.at[k], G.at[z, k], loc_sem.at[k])

    pl.semaphore_wait(barrier, 3 + has_r.astype(jnp.int32) + has_l.astype(jnp.int32))

    def column(block, core, k):
        return pl.multiple_of(block * (2 * K * w) + core * (K * w) + k * w - 64 * ((k + core) % 2), 128)

    def own_right(k):
        return remote(slab_ref.at[k], G.at[z, k], g_send.at[0, z, k], g_recv.at[z, k], right)

    def own_left(k):
        return remote(slab_ref.at[k], G.at[z, k], g_send.at[1, z, k], g_recv.at[z, k], left)

    def pass_right(block, k):
        return remote(G.at[block, k], G.at[block, k], g_send.at[0, block, k], g_recv.at[block, k], right)

    def pass_left(block, k):
        return remote(G.at[block, k], G.at[block, k], g_send.at[1, block, k], g_recv.at[block, k], left)

    def swap(block, k):
        return remote(
            pos_ref.at[:, pl.ds(column(block, 1 - c, k), win)], posin.at[block, k],
            p_send.at[block, k], p_recv.at[block, k], sib,
        )

    def send_q():
        return remote(q_ref, qb.at[1], q_send, q_recv, sib)

    def rows_of(slot, h, part):
        return RS.at[slot, h] if part is None else RS.at[slot, h, pl.ds(part * (w // 2), w // 2)]

    def sum_right(dest, h, part=None):
        src = rows_of(dest, h, part)
        return remote(src, src, r_send.at[dest, h], r_recv.at[dest, h], right)

    def sum_left(dest, h, part=None):
        slot = jnp.where(dest == z - 1, n, dest)
        return remote(rows_of(dest, h, part), rows_of(slot, h, part), r_send.at[dest, h], r_recv.at[slot, h], left)

    def arrived(slot, h):
        remote(RS.at[slot, h], RS.at[slot, h], r_send.at[0, 0], r_recv.at[slot, h], sib).wait_recv()

    @pl.loop(0, K)
    def _(k):
        @pl.when(has_r)
        def _():
            own_right(k).start()

        @pl.when(has_l)
        def _():
            own_left(k).start()

        @pl.when(k == 0)
        def _():
            send_q().start()

        local_slab(k).start()
        swap(z, k).start()

    q_own = pltpu.make_async_copy(q_ref, qb.at[0], loc_sem.at[K])
    q_own.start()

    @pl.loop(0, (n - 1) * K)
    def _(j):
        d, k = j // K + 1, j % K

        @pl.when(z + d < n)
        def _():
            swap(z + d, k).start()

        @pl.when(z - d >= 0)
        def _():
            swap(z - d, k).start()

    qacc[...] = jnp.zeros_like(qacc)
    q_own.wait()
    send_q().wait_recv()

    def marks_of(block, k):
        mine = pltpu.make_async_copy(pos_ref.at[:, pl.ds(column(block, c, k), win)], pt.at[0], pt_sem.at[0])
        theirs = pltpu.make_async_copy(posin.at[block, k], pt.at[1], pt_sem.at[1])
        return mine, theirs

    def fetch(block, k):
        mine, theirs = marks_of(block, k)
        mine.start()
        swap(block, k).wait_recv()
        theirs.start()

    def tile(block, k):
        for copy in marks_of(block, k):
            copy.wait()
        odd = (k + c) % 2 == 1

        @pl.loop(0, 2)
        def _(h):
            labels = G[block, k]
            logits = lax.dot_general(qb[h], labels, (((1,), (1,)), ((), ())), preferred_element_type=F32)
            marks = jnp.where(odd, pt[h, :, 64 : 64 + w], pt[h, :, 0:w]).astype(F32)
            grad = ((jax.nn.sigmoid(logits) - marks) * loss_weight).astype(BF16)
            gs[h] = grad
            qacc[h] += jnp.dot(grad, labels, preferred_element_type=F32)

        grads = gs[...].reshape(2 * rows, w)
        both = qb[...].reshape(2 * rows, D)
        part = lax.dot_general(grads, both, (((0,), (0,)), ((), ())), preferred_element_type=F32)
        PS[block, k] = part

    def turn(i, at):
        near_far = jnp.where(i < H, 1, jnp.where(i < 2 * H, 2, jnp.where(i < 3 * H, 3, 1)))
        near_h = i - jnp.where(i < H, H - NEAR, jnp.where(i < 2 * H, H, jnp.where(i < 3 * H, 2 * H, 3 * H - NEAR)))
        near_ok = (i >= H - NEAR) & (i < 4 * H - NEAR)
        m = i - NEAR
        mid_far = jnp.where((m >= 2 * H) & (m < 3 * H), 3, 2)
        mid_h = m - jnp.where(m < 2 * H, H, jnp.where(m < 3 * H, 2 * H, 3 * H - MID))
        mid_ok = (m >= H) & ((m < H + MID) | (m >= 2 * H)) & (m < 4 * H - MID)
        last_h = i - 2 * H - MID
        last_ok = (last_h >= 0) & (last_h < H)
        far = jnp.where(at == 0, near_far, jnp.where(at == 1, mid_far, 3))
        h = jnp.where(at == 0, near_h, jnp.where(at == 1, mid_h, last_h))
        ok = ((at == 0) & near_ok) | ((at == 1) & mid_ok) | ((at == 2) & last_ok)
        return far, h, ok

    def add(dest, h):
        arrived(dest, h)
        RS[dest, h] = (RS[dest, h].astype(F32) + PS[dest, h]).astype(BF16)

    def sent(i):
        for at, going_right in ((z, True), (zm, False)):
            far, h, ok = turn(i - LAG, at)
            dest = far if going_right else n - 1 - far

            @pl.when(ok)
            def _(dest=dest, h=h):
                sum_right(dest, h).wait_send()

    def sums(i):
        for at, going_right in ((z, True), (zm, False)):
            far, h, ok = turn(i, at)
            dest = far if going_right else n - 1 - far
            mid = 2 if going_right else n - 3
            send = sum_right if going_right else sum_left
            second = (at == 1) & (i == 3 * H + NEAR)

            @pl.when(ok & jnp.logical_not(second))
            def _(at=at, h=h, dest=dest, send=send):
                @pl.when(at > 0)
                def _():
                    add(dest, h)

                @pl.when(at == 0)
                def _():
                    RS[dest, h] = PS[dest, h].astype(BF16)

                send(dest, h).start()

            @pl.when((at == 1) & (i == H + NEAR + MID))
            def _(mid=mid, send=send):
                add(mid, MID)
                send(mid, MID, 0).start()

            @pl.when(second)
            def _(mid=mid, send=send):
                send(mid, MID, 1).start()

        sent(i)
        t = i - 3 * H

        @pl.when((t >= 0) & (t < H))
        def _():
            @pl.when(has_l)
            def _():
                arrived(z, t)
                PS[z, t] += RS[z, t].astype(F32)

            @pl.when(has_r)
            def _():
                arrived(n, t)
                PS[z, t] += RS[n, t].astype(F32)

            sout[t] = PS[z, t].astype(BF16)

    @pl.loop(0, (n - 1) * K)
    def _(j):
        d, k = j // K + 1, j % K

        @pl.when(j < K)
        def _():
            local_slab(k).wait()

        @pl.loop(0, 3)
        def _(s):
            block = jnp.where(s == 0, z, jnp.where(s == 1, z + d, z - d))
            busy = ((s == 0) & (j < K)) | ((s > 0) & (block >= 0) & (block < n))

            @pl.when(busy)
            def _():
                fetch(block, k)

            @pl.when((s == 1) & (block < n))
            def _():
                pass_left(block, k).wait_recv()

                @pl.when(has_l)
                def _():
                    pass_left(block, k).start()

            @pl.when((s == 2) & (block >= 0))
            def _():
                pass_right(block, k).wait_recv()

                @pl.when(has_r)
                def _():
                    pass_right(block, k).start()

            @pl.when(busy)
            def _():
                tile(block, k)

        sums(j)

    theirs = remote(qacc.at[1], qr, a_send, a_recv, sib)

    def over(stage, h):
        src = qacc.at[0, pl.ds(h * half, half)] if stage == 0 else xr.at[0, h]
        dev = partner[h] if stage == 0 else partner[1 - h]
        return remote(src, xr.at[stage, h], x_send.at[stage, h], x_recv.at[stage, h], dev)

    theirs.start()
    pl.loop(3 * H, 3 * H + 1)(sums)
    theirs.wait_recv()
    qacc[0] += qr[...]
    for h in range(2):
        over(0, h).start()
    send_q().wait_send()

    @pl.loop(0, n * K)
    def _(j):
        block, k = j // K, j % K
        swap(block, k).wait_send()

        @pl.when(has_r & (block <= z))
        def _():
            pass_right(block, k).wait_send()

        @pl.when(has_l & (block >= z))
        def _():
            pass_left(block, k).wait_send()

    pl.loop(3 * H + 1, 3 * H + H // 2)(sums)
    for h in range(2):
        over(0, h).wait_recv()
        xr[0, h] += qacc[0, h * half : (h + 1) * half, :]
        over(1, h).start()
    pl.loop(3 * H + H // 2, 4 * H - 1)(sums)
    theirs.wait_send()
    for h in range(2):
        over(0, h).wait_send()
    for h in range(2):
        over(1, h).wait_recv()
        qout[h * half : (h + 1) * half, :] = (xr[0, h] + xr[1, h]).astype(BF16)
    pl.loop(4 * H - 1, 4 * H)(sums)

    for h in range(2):
        over(1, h).wait_send()

    @pl.loop(4 * H, 4 * H + LAG)
    def _(i):
        sent(i)


def copy_kernel(q_ref, s_ref, q_out, s_out, sem):
    copies = [pltpu.make_async_copy(q_ref, q_out, sem.at[0])]
    copies.append(pltpu.make_async_copy(s_ref, s_out, sem.at[1]))
    for copy in copies:
        copy.start()
    for copy in copies:
        copy.wait()


def hand_over(query_grad, slab_grad):
    vmem = pl.BlockSpec(memory_space=pltpu.VMEM)
    hbm = pl.BlockSpec(memory_space=pl.ANY)
    return pl.pallas_call(
        copy_kernel,
        out_shape=tuple(jax.ShapeDtypeStruct(x.shape, x.dtype) for x in (query_grad, slab_grad)),
        in_specs=[vmem, vmem],
        compiler_params=pltpu.CompilerParams(vmem_limit_bytes=2**20),
        out_specs=(hbm, hbm),
        scratch_shapes=[pltpu.SemaphoreType.DMA((slab_grad.shape[0] + 1,))],
    )(*(pltpu.with_memory_space_constraint(x, pltpu.VMEM) for x in (query_grad, slab_grad)))


def fused(n, queries, slab, positives):
    rows, D = queries.shape
    R = slab.shape[0]
    K, w = PARTS, R // PARTS
    win = w + 64
    vmem = pl.BlockSpec(memory_space=pltpu.VMEM)
    hbm = pl.BlockSpec(memory_space=pl.ANY)
    dma = pltpu.SemaphoreType.DMA
    query_grad, slab_grad, _ = pl.pallas_call(
        lambda *refs: line_kernel(n, win, *refs),
        out_shape=(
            pltpu.VMEM((rows, D), BF16),
            pltpu.VMEM((K, w, D), BF16),
            jax.ShapeDtypeStruct((n, K, rows, win), jnp.int32),
        ),
        in_specs=[hbm, hbm, hbm],
        out_specs=(vmem, vmem, hbm),
        scratch_shapes=[
            pltpu.VMEM((n, K, w, D), BF16),
            pltpu.VMEM((n + 1, K, w, D), BF16),
            pltpu.VMEM((n, K, w, D), F32),
            pltpu.VMEM((2, rows, D), BF16),
            pltpu.VMEM((2, rows, D), F32),
            pltpu.VMEM((2, rows, win), jnp.int32),
            pltpu.VMEM((2, rows, w), BF16),
            pltpu.VMEM((rows, D), F32),
            pltpu.VMEM((2, 2, rows // 2, D), F32),
            dma((K + 1,)), dma, dma, dma((n, K)), dma((n, K)), dma((2,)),
            dma((2, n, K)), dma((n, K)), dma((n, K)), dma((n + 1, K)), dma, dma, dma((2, 2)), dma((2, 2)),
        ],
        compiler_params=pltpu.CompilerParams(
            collective_id=0, has_side_effects=True, vmem_limit_bytes=58 * 2**20
        ),
        cost_estimate=pl.CostEstimate(
            flops=12 * rows * n * R * D, bytes_accessed=rows * n * R * 8, transcendentals=2 * rows * n * R
        ),
    )(queries, slab.reshape(K, w, D), positives)
    query_grad, slab_grad = hand_over(query_grad, slab_grad)
    return query_grad, slab_grad.reshape(R, D)


def solution(mesh):
    labels, batch = mesh.shape["label"], mesh.shape["batch"]

    def per_device(queries, slab, positives):
        R = slab.shape[0]
        fits = labels == 4 and batch == 8 and R % (PARTS * 64) == 0 and (R // PARTS) % 128 == 64
        if fits and (R // 64) % 2 == 1 and queries.shape[0] % 32 == 0 and R <= 1600:
            return fused(batch // 2, queries, slab, positives)
        return plain(queries, slab, positives)

    return jax.shard_map(
        per_device,
        mesh=mesh,
        in_specs=(P("batch", None), P(("label", "batch"), None), P("batch", "label")),
        out_specs=(P("batch", None), P(("label", "batch"), None)),
        check_vma=False,
    )
```

```python
import jax
import jax.numpy as jnp
from jax import lax
from jax.experimental import pallas as pl
from jax.experimental.pallas import tpu as pltpu
from jax.sharding import PartitionSpec as P

loss_weight = 0.0625
MESH = pl.DeviceIdType.MESH
F32, BF16 = jnp.float32, jnp.bfloat16
PARTS = 5
NEAR, MID, LAG, LEAD = 2, 3, 5, 2


def plain(queries, slab, positives):
    piece = lax.all_gather(slab, "batch", axis=0, tiled=True)
    logits = lax.dot_general(queries, piece, (((1,), (1,)), ((), ())), preferred_element_type=F32)
    grad = ((jax.nn.sigmoid(logits) - positives.astype(F32)) * loss_weight).astype(BF16)
    query_grad = lax.psum(jnp.dot(grad, piece, preferred_element_type=F32), "label").astype(BF16)
    slab_grad = lax.psum_scatter(
        lax.dot_general(grad, queries, (((0,), (0,)), ((), ())), preferred_element_type=F32),
        "batch",
        scatter_dimension=0,
        tiled=True,
    ).astype(BF16)
    return query_grad, slab_grad


def remote(src, dst, send, recv, device):
    return pltpu.make_async_remote_copy(
        src_ref=src, dst_ref=dst, send_sem=send, recv_sem=recv, device_id=device, device_id_type=MESH
    )


def line_kernel(
    n, win,
    q_ref, slab_ref, pos_ref,
    qout, sout, posin,
    G, RS, PS, qb, qacc, pt, gs, qr, xr,
    loc_sem, q_send, q_recv, p_send, p_recv, pt_sem, g_send, g_recv, r_send, r_recv, a_send, a_recv, x_send, x_recv,
):
    K, w, D = slab_ref.shape
    H = K
    rows = q_ref.shape[0]
    half = rows // 2
    l = lax.axis_index("label")
    b = lax.axis_index("batch")
    z, c = b // 2, b % 2
    zm = n - 1 - z
    sib = {"batch": b + 1 - 2 * c}
    right, left = {"batch": b + 2}, {"batch": b - 2}
    partner = ({"label": l + 1 - 2 * (l % 2)}, {"label": l + 2 - 4 * (l // 2)})
    has_r, has_l = z < n - 1, z > 0

    barrier = pltpu.get_barrier_semaphore()
    for dev in (sib, *partner):
        pl.semaphore_signal(barrier, inc=1, device_id=dev, device_id_type=MESH)

    @pl.when(has_r)
    def _():
        pl.semaphore_signal(barrier, inc=1, device_id=right, device_id_type=MESH)

    @pl.when(has_l)
    def _():
        pl.semaphore_signal(barrier, inc=1, device_id=left, device_id_type=MESH)

    def local_slab(k):
        return pltpu.make_async_copy(slab_ref.at[k], G.at[z, k], loc_sem.at[k])

    pl.semaphore_wait(barrier, 3 + has_r.astype(jnp.int32) + has_l.astype(jnp.int32))

    def column(block, core, k):
        return pl.multiple_of(block * (2 * K * w) + core * (K * w) + k * w - 64 * ((k + core) % 2), 128)

    def own_right(k):
        return remote(slab_ref.at[k], G.at[z, k], g_send.at[0, z, k], g_recv.at[z, k], right)

    def own_left(k):
        return remote(slab_ref.at[k], G.at[z, k], g_send.at[1, z, k], g_recv.at[z, k], left)

    def pass_right(block, k):
        return remote(G.at[block, k], G.at[block, k], g_send.at[0, block, k], g_recv.at[block, k], right)

    def pass_left(block, k):
        return remote(G.at[block, k], G.at[block, k], g_send.at[1, block, k], g_recv.at[block, k], left)

    def swap(block, k):
        return remote(
            pos_ref.at[:, pl.ds(column(block, 1 - c, k), win)], posin.at[block, k],
            p_send.at[block, k], p_recv.at[block, k], sib,
        )

    def send_q():
        return remote(q_ref, qb.at[1], q_send, q_recv, sib)

    def rows_of(slot, h, part):
        return RS.at[slot, h] if part is None else RS.at[slot, h, pl.ds(part * (w // 2), w // 2)]

    def sum_right(dest, h, part=None):
        src = rows_of(dest, h, part)
        return remote(src, src, r_send.at[dest, h], r_recv.at[dest, h], right)

    def sum_left(dest, h, part=None):
        slot = jnp.where(dest == z - 1, n, dest)
        return remote(rows_of(dest, h, part), rows_of(slot, h, part), r_send.at[dest, h], r_recv.at[slot, h], left)

    def arrived(slot, h):
        remote(RS.at[slot, h], RS.at[slot, h], r_send.at[0, 0], r_recv.at[slot, h], sib).wait_recv()

    @pl.loop(0, K)
    def _(k):
        @pl.when(has_r)
        def _():
            own_right(k).start()

        @pl.when(has_l)
        def _():
            own_left(k).start()

        @pl.when(k == 0)
        def _():
            send_q().start()

        local_slab(k).start()

    q_own = pltpu.make_async_copy(q_ref, qb.at[0], loc_sem.at[K])
    q_own.start()

    def swaps(j):
        d, k = j // K + 1, j % K

        @pl.when(j < K)
        def _():
            swap(z, k).start()

        @pl.when((j < (n - 1) * K) & (z + d < n))
        def _():
            swap(z + d, k).start()

        @pl.when((j < (n - 1) * K) & (z - d >= 0))
        def _():
            swap(z - d, k).start()

    pl.loop(0, LEAD)(swaps)
    qacc[...] = jnp.zeros_like(qacc)
    q_own.wait()
    send_q().wait_recv()

    def marks_of(block, k):
        mine = pltpu.make_async_copy(pos_ref.at[:, pl.ds(column(block, c, k), win)], pt.at[0], pt_sem.at[0])
        theirs = pltpu.make_async_copy(posin.at[block, k], pt.at[1], pt_sem.at[1])
        return mine, theirs

    def fetch(block, k):
        mine, theirs = marks_of(block, k)
        mine.start()
        swap(block, k).wait_recv()
        theirs.start()

    def tile(block, k):
        for copy in marks_of(block, k):
            copy.wait()
        odd = (k + c) % 2 == 1

        @pl.loop(0, 2)
        def _(h):
            labels = G[block, k]
            logits = lax.dot_general(qb[h], labels, (((1,), (1,)), ((), ())), preferred_element_type=F32)
            marks = jnp.where(odd, pt[h, :, 64 : 64 + w], pt[h, :, 0:w]).astype(F32)
            grad = ((jax.nn.sigmoid(logits) - marks) * loss_weight).astype(BF16)
            gs[h] = grad
            qacc[h] += jnp.dot(grad, labels, preferred_element_type=F32)

        grads = gs[...].reshape(2 * rows, w)
        both = qb[...].reshape(2 * rows, D)
        part = lax.dot_general(grads, both, (((0,), (0,)), ((), ())), preferred_element_type=F32)
        PS[block, k] = part

    def turn(i, at):
        near_far = jnp.where(i < H, 1, jnp.where(i < 2 * H, 2, jnp.where(i < 3 * H, 3, 1)))
        near_h = i - jnp.where(i < H, H - NEAR, jnp.where(i < 2 * H, H, jnp.where(i < 3 * H, 2 * H, 3 * H - NEAR)))
        near_ok = (i >= H - NEAR) & (i < 4 * H - NEAR)
        m = i - NEAR
        mid_far = jnp.where((m >= 2 * H) & (m < 3 * H), 3, 2)
        mid_h = m - jnp.where(m < 2 * H, H, jnp.where(m < 3 * H, 2 * H, 3 * H - MID))
        mid_ok = (m >= H) & ((m < H + MID) | (m >= 2 * H)) & (m < 4 * H - MID)
        last_h = i - 2 * H - MID
        last_ok = (last_h >= 0) & (last_h < H)
        far = jnp.where(at == 0, near_far, jnp.where(at == 1, mid_far, 3))
        h = jnp.where(at == 0, near_h, jnp.where(at == 1, mid_h, last_h))
        ok = ((at == 0) & near_ok) | ((at == 1) & mid_ok) | ((at == 2) & last_ok)
        return far, h, ok

    def add(dest, h):
        arrived(dest, h)
        RS[dest, h] = (RS[dest, h].astype(F32) + PS[dest, h]).astype(BF16)

    def sent(i):
        for at, going_right in ((z, True), (zm, False)):
            far, h, ok = turn(i - LAG, at)
            dest = far if going_right else n - 1 - far

            @pl.when(ok)
            def _(dest=dest, h=h):
                sum_right(dest, h).wait_send()

    def sums(i):
        for at, going_right in ((z, True), (zm, False)):
            far, h, ok = turn(i, at)
            dest = far if going_right else n - 1 - far
            mid = 2 if going_right else n - 3
            send = sum_right if going_right else sum_left
            second = (at == 1) & (i == 3 * H + NEAR)

            @pl.when(ok & jnp.logical_not(second))
            def _(at=at, h=h, dest=dest, send=send):
                @pl.when(at > 0)
                def _():
                    add(dest, h)

                @pl.when(at == 0)
                def _():
                    RS[dest, h] = PS[dest, h].astype(BF16)

                send(dest, h).start()

            @pl.when((at == 1) & (i == H + NEAR + MID))
            def _(mid=mid, send=send):
                add(mid, MID)
                send(mid, MID, 0).start()

            @pl.when(second)
            def _(mid=mid, send=send):
                send(mid, MID, 1).start()

        sent(i)
        t = i - 3 * H

        @pl.when((t >= 0) & (t < H))
        def _():
            @pl.when(has_l)
            def _():
                arrived(z, t)

            @pl.when(has_r)
            def _():
                arrived(n, t)

            @pl.when(has_l & has_r)
            def _():
                sout[t] = (PS[z, t] + RS[z, t].astype(F32) + RS[n, t].astype(F32)).astype(BF16)

            @pl.when(has_l & jnp.logical_not(has_r))
            def _():
                sout[t] = (PS[z, t] + RS[z, t].astype(F32)).astype(BF16)

            @pl.when(has_r & jnp.logical_not(has_l))
            def _():
                sout[t] = (PS[z, t] + RS[n, t].astype(F32)).astype(BF16)

    @pl.loop(0, (n - 1) * K)
    def _(j):
        d, k = j // K + 1, j % K
        swaps(j + LEAD)

        @pl.when(j < K)
        def _():
            local_slab(k).wait()

        @pl.loop(0, 3)
        def _(s):
            block = jnp.where(s == 0, z, jnp.where(s == 1, z + d, z - d))
            busy = ((s == 0) & (j < K)) | ((s > 0) & (block >= 0) & (block < n))

            @pl.when(busy)
            def _():
                fetch(block, k)

            @pl.when((s == 1) & (block < n))
            def _():
                pass_left(block, k).wait_recv()

                @pl.when(has_l)
                def _():
                    pass_left(block, k).start()

            @pl.when((s == 2) & (block >= 0))
            def _():
                pass_right(block, k).wait_recv()

                @pl.when(has_r)
                def _():
                    pass_right(block, k).start()

            @pl.when(busy)
            def _():
                tile(block, k)

        sums(j)

    theirs = remote(qacc.at[1], qr, a_send, a_recv, sib)

    def over(stage, h):
        src = qacc.at[0, pl.ds(h * half, half)] if stage == 0 else xr.at[0, h]
        dev = partner[h] if stage == 0 else partner[1 - h]
        return remote(src, xr.at[stage, h], x_send.at[stage, h], x_recv.at[stage, h], dev)

    theirs.start()
    pl.loop(3 * H, 3 * H + 1)(sums)
    theirs.wait_recv()
    qacc[0] += qr[...]
    for h in range(2):
        over(0, h).start()
    send_q().wait_send()

    @pl.loop(0, n * K)
    def _(j):
        block, k = j // K, j % K
        swap(block, k).wait_send()

        @pl.when(has_r & (block <= z))
        def _():
            pass_right(block, k).wait_send()

        @pl.when(has_l & (block >= z))
        def _():
            pass_left(block, k).wait_send()

    pl.loop(3 * H + 1, 3 * H + H // 2)(sums)
    for h in range(2):
        over(0, h).wait_recv()
        xr[0, h] += qacc[0, h * half : (h + 1) * half, :]
        over(1, h).start()
    pl.loop(3 * H + H // 2, 4 * H - 1)(sums)
    theirs.wait_send()
    for h in range(2):
        over(0, h).wait_send()
    for h in range(2):
        over(1, h).wait_recv()
        qout[h * half : (h + 1) * half, :] = (xr[0, h] + xr[1, h]).astype(BF16)
    pl.loop(4 * H - 1, 4 * H)(sums)

    for h in range(2):
        over(1, h).wait_send()

    @pl.loop(4 * H, 4 * H + LAG)
    def _(i):
        sent(i)


def copy_kernel(q_ref, s_ref, q_out, s_out, sem):
    copies = [pltpu.make_async_copy(q_ref, q_out, sem.at[0])]
    copies.append(pltpu.make_async_copy(s_ref, s_out, sem.at[1]))
    for copy in copies:
        copy.start()
    for copy in copies:
        copy.wait()


def hand_over(query_grad, slab_grad):
    vmem = pl.BlockSpec(memory_space=pltpu.VMEM)
    hbm = pl.BlockSpec(memory_space=pl.ANY)
    return pl.pallas_call(
        copy_kernel,
        out_shape=tuple(jax.ShapeDtypeStruct(x.shape, x.dtype) for x in (query_grad, slab_grad)),
        in_specs=[vmem, vmem],
        compiler_params=pltpu.CompilerParams(vmem_limit_bytes=2**20),
        out_specs=(hbm, hbm),
        scratch_shapes=[pltpu.SemaphoreType.DMA((slab_grad.shape[0] + 1,))],
    )(*(pltpu.with_memory_space_constraint(x, pltpu.VMEM) for x in (query_grad, slab_grad)))


def fused(n, queries, slab, positives):
    rows, D = queries.shape
    R = slab.shape[0]
    K, w = PARTS, R // PARTS
    win = w + 64
    vmem = pl.BlockSpec(memory_space=pltpu.VMEM)
    hbm = pl.BlockSpec(memory_space=pl.ANY)
    dma = pltpu.SemaphoreType.DMA
    query_grad, slab_grad, _ = pl.pallas_call(
        lambda *refs: line_kernel(n, win, *refs),
        out_shape=(
            pltpu.VMEM((rows, D), BF16),
            pltpu.VMEM((K, w, D), BF16),
            jax.ShapeDtypeStruct((n, K, rows, win), jnp.int32),
        ),
        in_specs=[hbm, hbm, hbm],
        out_specs=(vmem, vmem, hbm),
        scratch_shapes=[
            pltpu.VMEM((n, K, w, D), BF16),
            pltpu.VMEM((n + 1, K, w, D), BF16),
            pltpu.VMEM((n, K, w, D), F32),
            pltpu.VMEM((2, rows, D), BF16),
            pltpu.VMEM((2, rows, D), F32),
            pltpu.VMEM((2, rows, win), jnp.int32),
            pltpu.VMEM((2, rows, w), BF16),
            pltpu.VMEM((rows, D), F32),
            pltpu.VMEM((2, 2, rows // 2, D), F32),
            dma((K + 1,)), dma, dma, dma((n, K)), dma((n, K)), dma((2,)),
            dma((2, n, K)), dma((n, K)), dma((n, K)), dma((n + 1, K)), dma, dma, dma((2, 2)), dma((2, 2)),
        ],
        compiler_params=pltpu.CompilerParams(
            collective_id=0, has_side_effects=True, vmem_limit_bytes=58 * 2**20
        ),
        cost_estimate=pl.CostEstimate(
            flops=12 * rows * n * R * D, bytes_accessed=rows * n * R * 8, transcendentals=2 * rows * n * R
        ),
    )(queries, slab.reshape(K, w, D), positives)
    query_grad, slab_grad = hand_over(query_grad, slab_grad)
    return query_grad, slab_grad.reshape(R, D)


def solution(mesh):
    labels, batch = mesh.shape["label"], mesh.shape["batch"]

    def per_device(queries, slab, positives):
        R = slab.shape[0]
        fits = labels == 4 and batch == 8 and R % (PARTS * 64) == 0 and (R // PARTS) % 128 == 64
        if fits and (R // 64) % 2 == 1 and queries.shape[0] % 32 == 0 and R <= 1600:
            return fused(batch // 2, queries, slab, positives)
        return plain(queries, slab, positives)

    return jax.shard_map(
        per_device,
        mesh=mesh,
        in_specs=(P("batch", None), P(("label", "batch"), None), P("batch", "label")),
        out_specs=(P("batch", None), P(("label", "batch"), None)),
        check_vma=False,
    )
```

```python
import jax
import jax.numpy as jnp
from jax import lax
from jax.experimental import pallas as pl
from jax.experimental.pallas import tpu as pltpu
from jax.sharding import PartitionSpec as P

loss_weight = 0.0625
MESH = pl.DeviceIdType.MESH
F32, BF16 = jnp.float32, jnp.bfloat16
PARTS = 5
NEAR, MID, LAG, LEAD = 2, 3, 5, 2


def plain(queries, slab, positives):
    piece = lax.all_gather(slab, "batch", axis=0, tiled=True)
    logits = lax.dot_general(queries, piece, (((1,), (1,)), ((), ())), preferred_element_type=F32)
    grad = ((jax.nn.sigmoid(logits) - positives.astype(F32)) * loss_weight).astype(BF16)
    query_grad = lax.psum(jnp.dot(grad, piece, preferred_element_type=F32), "label").astype(BF16)
    slab_grad = lax.psum_scatter(
        lax.dot_general(grad, queries, (((0,), (0,)), ((), ())), preferred_element_type=F32),
        "batch",
        scatter_dimension=0,
        tiled=True,
    ).astype(BF16)
    return query_grad, slab_grad


def remote(src, dst, send, recv, device):
    return pltpu.make_async_remote_copy(
        src_ref=src, dst_ref=dst, send_sem=send, recv_sem=recv, device_id=device, device_id_type=MESH
    )


def line_kernel(
    n, win,
    q_ref, slab_ref, pos_ref,
    qout, sout, posin,
    G, RS, PS, qb, qacc, pt, gs, qr, xr,
    loc_sem, q_send, q_recv, p_send, p_recv, pt_sem, g_send, g_recv, r_send, r_recv, a_send, a_recv, x_send, x_recv,
):
    K, w, D = slab_ref.shape
    H = K
    rows = q_ref.shape[0]
    half = rows // 2
    l = lax.axis_index("label")
    b = lax.axis_index("batch")
    z, c = b // 2, b % 2
    zm = n - 1 - z
    sib = {"batch": b + 1 - 2 * c}
    right, left = {"batch": b + 2}, {"batch": b - 2}
    partner = ({"label": l + 1 - 2 * (l % 2)}, {"label": l + 2 - 4 * (l // 2)})
    has_r, has_l = z < n - 1, z > 0

    barrier = pltpu.get_barrier_semaphore()
    for dev in (sib, *partner):
        pl.semaphore_signal(barrier, inc=1, device_id=dev, device_id_type=MESH)

    @pl.when(has_r)
    def _():
        pl.semaphore_signal(barrier, inc=1, device_id=right, device_id_type=MESH)

    @pl.when(has_l)
    def _():
        pl.semaphore_signal(barrier, inc=1, device_id=left, device_id_type=MESH)

    def local_slab(k):
        return pltpu.make_async_copy(slab_ref.at[k], G.at[z, k], loc_sem.at[k])

    pl.semaphore_wait(barrier, 3 + has_r.astype(jnp.int32) + has_l.astype(jnp.int32))

    def column(block, core, k):
        return pl.multiple_of(block * (2 * K * w) + core * (K * w) + k * w - 64 * ((k + core) % 2), 128)

    def own_right(k):
        return remote(slab_ref.at[k], G.at[z, k], g_send.at[0, z, k], g_recv.at[z, k], right)

    def own_left(k):
        return remote(slab_ref.at[k], G.at[z, k], g_send.at[1, z, k], g_recv.at[z, k], left)

    def pass_right(block, k):
        return remote(G.at[block, k], G.at[block, k], g_send.at[0, block, k], g_recv.at[block, k], right)

    def pass_left(block, k):
        return remote(G.at[block, k], G.at[block, k], g_send.at[1, block, k], g_recv.at[block, k], left)

    def swap(block, k):
        return remote(
            pos_ref.at[:, pl.ds(column(block, 1 - c, k), win)], posin.at[block, k],
            p_send.at[block, k], p_recv.at[block, k], sib,
        )

    def send_q():
        return remote(q_ref, qb.at[1], q_send, q_recv, sib)

    def rows_of(slot, h, part):
        return RS.at[slot, h] if part is None else RS.at[slot, h, pl.ds(part * (w // 2), w // 2)]

    def sum_right(dest, h, part=None):
        src = rows_of(dest, h, part)
        return remote(src, src, r_send.at[dest, h], r_recv.at[dest, h], right)

    def sum_left(dest, h, part=None):
        slot = jnp.where(dest == z - 1, n, dest)
        return remote(rows_of(dest, h, part), rows_of(slot, h, part), r_send.at[dest, h], r_recv.at[slot, h], left)

    def arrived(slot, h):
        remote(RS.at[slot, h], RS.at[slot, h], r_send.at[0, 0], r_recv.at[slot, h], sib).wait_recv()

    @pl.loop(0, K)
    def _(k):
        @pl.when(has_r)
        def _():
            own_right(k).start()

        @pl.when(has_l)
        def _():
            own_left(k).start()

        @pl.when(k == 0)
        def _():
            send_q().start()

        local_slab(k).start()

    q_own = pltpu.make_async_copy(q_ref, qb.at[0], loc_sem.at[K])
    q_own.start()

    def swaps(j):
        d, k = j // K + 1, j % K

        @pl.when(j < K)
        def _():
            swap(z, k).start()

        @pl.when((j < (n - 1) * K) & (z + d < n))
        def _():
            swap(z + d, k).start()

        @pl.when((j < (n - 1) * K) & (z - d >= 0))
        def _():
            swap(z - d, k).start()

    pl.loop(0, LEAD)(swaps)
    qacc[...] = jnp.zeros_like(qacc)
    q_own.wait()
    send_q().wait_recv()

    def marks_of(block, k):
        mine = pltpu.make_async_copy(pos_ref.at[:, pl.ds(column(block, c, k), win)], pt.at[0], pt_sem.at[0])
        theirs = pltpu.make_async_copy(posin.at[block, k], pt.at[1], pt_sem.at[1])
        return mine, theirs

    def fetch(block, k):
        mine, theirs = marks_of(block, k)
        mine.start()
        swap(block, k).wait_recv()
        theirs.start()

    def tile(block, k):
        for copy in marks_of(block, k):
            copy.wait()
        odd = (k + c) % 2 == 1

        @pl.loop(0, 2)
        def _(h):
            labels = G[block, k]
            logits = lax.dot_general(qb[h], labels, (((1,), (1,)), ((), ())), preferred_element_type=F32)
            marks = jnp.where(odd, pt[h, :, 64 : 64 + w], pt[h, :, 0:w]).astype(F32)
            grad = ((jax.nn.sigmoid(logits) - marks) * loss_weight).astype(BF16)
            gs[h] = grad
            qacc[h] += jnp.dot(grad, labels, preferred_element_type=F32)

        grads = gs[...].reshape(2 * rows, w)
        both = qb[...].reshape(2 * rows, D)
        part = lax.dot_general(grads, both, (((0,), (0,)), ((), ())), preferred_element_type=F32)
        PS[block, k] = part

    def turn(i, at):
        near_far = jnp.where(i < H, 1, jnp.where(i < 2 * H, 2, jnp.where(i < 3 * H, 3, 1)))
        near_h = i - jnp.where(i < H, H - NEAR, jnp.where(i < 2 * H, H, jnp.where(i < 3 * H, 2 * H, 3 * H - NEAR)))
        near_ok = (i >= H - NEAR) & (i < 4 * H - NEAR)
        m = i - NEAR
        mid_far = jnp.where((m >= 2 * H) & (m < 3 * H), 3, 2)
        mid_h = m - jnp.where(m < 2 * H, H, jnp.where(m < 3 * H, 2 * H, 3 * H - MID))
        mid_ok = (m >= H) & ((m < H + MID) | (m >= 2 * H)) & (m < 4 * H - MID)
        last_h = i - 2 * H - MID
        last_ok = (last_h >= 0) & (last_h < H)
        far = jnp.where(at == 0, near_far, jnp.where(at == 1, mid_far, 3))
        h = jnp.where(at == 0, near_h, jnp.where(at == 1, mid_h, last_h))
        ok = ((at == 0) & near_ok) | ((at == 1) & mid_ok) | ((at == 2) & last_ok)
        return far, h, ok

    def add(dest, h):
        arrived(dest, h)
        RS[dest, h] = (RS[dest, h].astype(F32) + PS[dest, h]).astype(BF16)

    def sent(i):
        for at, going_right in ((z, True), (zm, False)):
            far, h, ok = turn(i - LAG, at)
            dest = far if going_right else n - 1 - far

            @pl.when(ok)
            def _(dest=dest, h=h):
                sum_right(dest, h).wait_send()

    def sums(i):
        for at, going_right in ((z, True), (zm, False)):
            far, h, ok = turn(i, at)
            dest = far if going_right else n - 1 - far
            mid = 2 if going_right else n - 3
            send = sum_right if going_right else sum_left
            second = (at == 1) & (i == 3 * H + NEAR)

            @pl.when(ok & (at < 2) & jnp.logical_not(second))
            def _(at=at, h=h, dest=dest, send=send):
                @pl.when(at == 1)
                def _():
                    add(dest, h)

                @pl.when(at == 0)
                def _():
                    RS[dest, h] = PS[dest, h].astype(BF16)

                send(dest, h).start()

            @pl.when((at == 1) & (i == H + NEAR + MID))
            def _(mid=mid, send=send):
                add(mid, MID)
                send(mid, MID, 0).start()

            @pl.when(second)
            def _(mid=mid, send=send):
                send(mid, MID, 1).start()

        for at, going_right in ((z, True), (zm, False)):
            far, h, ok = turn(i, at)
            dest = far if going_right else n - 1 - far
            send = sum_right if going_right else sum_left

            @pl.when(ok & (at == 2))
            def _(h=h, dest=dest, send=send):
                add(dest, h)
                send(dest, h).start()

        sent(i)
        t = i - 3 * H

        @pl.when((t >= 0) & (t < H))
        def _():
            @pl.when(has_l)
            def _():
                arrived(z, t)

            @pl.when(has_r)
            def _():
                arrived(n, t)

            @pl.when(has_l & has_r)
            def _():
                sout[t] = (PS[z, t] + RS[z, t].astype(F32) + RS[n, t].astype(F32)).astype(BF16)

            @pl.when(has_l & jnp.logical_not(has_r))
            def _():
                sout[t] = (PS[z, t] + RS[z, t].astype(F32)).astype(BF16)

            @pl.when(has_r & jnp.logical_not(has_l))
            def _():
                sout[t] = (PS[z, t] + RS[n, t].astype(F32)).astype(BF16)

    @pl.loop(0, (n - 1) * K)
    def _(j):
        d, k = j // K + 1, j % K
        swaps(j + LEAD)

        @pl.when(j < K)
        def _():
            local_slab(k).wait()

        @pl.loop(0, 3)
        def _(s):
            block = jnp.where(s == 0, z, jnp.where(s == 1, z + d, z - d))
            busy = ((s == 0) & (j < K)) | ((s > 0) & (block >= 0) & (block < n))

            @pl.when(busy)
            def _():
                fetch(block, k)

            @pl.when((s == 1) & (block < n))
            def _():
                pass_left(block, k).wait_recv()

                @pl.when(has_l)
                def _():
                    pass_left(block, k).start()

            @pl.when((s == 2) & (block >= 0))
            def _():
                pass_right(block, k).wait_recv()

                @pl.when(has_r)
                def _():
                    pass_right(block, k).start()

            @pl.when(busy)
            def _():
                tile(block, k)

        sums(j)

    theirs = remote(qacc.at[1], qr, a_send, a_recv, sib)

    def over(stage, h):
        src = qacc.at[0, pl.ds(h * half, half)] if stage == 0 else xr.at[0, h]
        dev = partner[h] if stage == 0 else partner[1 - h]
        return remote(src, xr.at[stage, h], x_send.at[stage, h], x_recv.at[stage, h], dev)

    theirs.start()
    pl.loop(3 * H, 3 * H + 1)(sums)
    theirs.wait_recv()
    qacc[0] += qr[...]
    for h in range(2):
        over(0, h).start()
    send_q().wait_send()

    @pl.loop(0, n * K)
    def _(j):
        block, k = j // K, j % K
        swap(block, k).wait_send()

        @pl.when(has_r & (block <= z))
        def _():
            pass_right(block, k).wait_send()

        @pl.when(has_l & (block >= z))
        def _():
            pass_left(block, k).wait_send()

    pl.loop(3 * H + 1, 3 * H + H // 2)(sums)
    for h in range(2):
        over(0, h).wait_recv()
        xr[0, h] += qacc[0, h * half : (h + 1) * half, :]
        over(1, h).start()
    pl.loop(3 * H + H // 2, 4 * H - 1)(sums)
    theirs.wait_send()
    for h in range(2):
        over(0, h).wait_send()
    for h in range(2):
        over(1, h).wait_recv()
        qout[h * half : (h + 1) * half, :] = (xr[0, h] + xr[1, h]).astype(BF16)
    pl.loop(4 * H - 1, 4 * H)(sums)

    for h in range(2):
        over(1, h).wait_send()

    @pl.loop(4 * H, 4 * H + LAG)
    def _(i):
        sent(i)


def copy_kernel(q_ref, s_ref, q_out, s_out, sem):
    copies = [pltpu.make_async_copy(q_ref, q_out, sem.at[0])]
    copies.append(pltpu.make_async_copy(s_ref, s_out, sem.at[1]))
    for copy in copies:
        copy.start()
    for copy in copies:
        copy.wait()


def hand_over(query_grad, slab_grad):
    vmem = pl.BlockSpec(memory_space=pltpu.VMEM)
    hbm = pl.BlockSpec(memory_space=pl.ANY)
    return pl.pallas_call(
        copy_kernel,
        out_shape=tuple(jax.ShapeDtypeStruct(x.shape, x.dtype) for x in (query_grad, slab_grad)),
        in_specs=[vmem, vmem],
        compiler_params=pltpu.CompilerParams(vmem_limit_bytes=2**20),
        out_specs=(hbm, hbm),
        scratch_shapes=[pltpu.SemaphoreType.DMA((slab_grad.shape[0] + 1,))],
    )(*(pltpu.with_memory_space_constraint(x, pltpu.VMEM) for x in (query_grad, slab_grad)))


def fused(n, queries, slab, positives):
    rows, D = queries.shape
    R = slab.shape[0]
    K, w = PARTS, R // PARTS
    win = w + 64
    vmem = pl.BlockSpec(memory_space=pltpu.VMEM)
    hbm = pl.BlockSpec(memory_space=pl.ANY)
    dma = pltpu.SemaphoreType.DMA
    query_grad, slab_grad, _ = pl.pallas_call(
        lambda *refs: line_kernel(n, win, *refs),
        out_shape=(
            pltpu.VMEM((rows, D), BF16),
            pltpu.VMEM((K, w, D), BF16),
            jax.ShapeDtypeStruct((n, K, rows, win), jnp.int32),
        ),
        in_specs=[hbm, hbm, hbm],
        out_specs=(vmem, vmem, hbm),
        scratch_shapes=[
            pltpu.VMEM((n, K, w, D), BF16),
            pltpu.VMEM((n + 1, K, w, D), BF16),
            pltpu.VMEM((n, K, w, D), F32),
            pltpu.VMEM((2, rows, D), BF16),
            pltpu.VMEM((2, rows, D), F32),
            pltpu.VMEM((2, rows, win), jnp.int32),
            pltpu.VMEM((2, rows, w), BF16),
            pltpu.VMEM((rows, D), F32),
            pltpu.VMEM((2, 2, rows // 2, D), F32),
            dma((K + 1,)), dma, dma, dma((n, K)), dma((n, K)), dma((2,)),
            dma((2, n, K)), dma((n, K)), dma((n, K)), dma((n + 1, K)), dma, dma, dma((2, 2)), dma((2, 2)),
        ],
        compiler_params=pltpu.CompilerParams(
            collective_id=0, has_side_effects=True, vmem_limit_bytes=58 * 2**20
        ),
        cost_estimate=pl.CostEstimate(
            flops=12 * rows * n * R * D, bytes_accessed=rows * n * R * 8, transcendentals=2 * rows * n * R
        ),
    )(queries, slab.reshape(K, w, D), positives)
    query_grad, slab_grad = hand_over(query_grad, slab_grad)
    return query_grad, slab_grad.reshape(R, D)


def solution(mesh):
    labels, batch = mesh.shape["label"], mesh.shape["batch"]

    def per_device(queries, slab, positives):
        R = slab.shape[0]
        fits = labels == 4 and batch == 8 and R % (PARTS * 64) == 0 and (R // PARTS) % 128 == 64
        if fits and (R // 64) % 2 == 1 and queries.shape[0] % 32 == 0 and R <= 1600:
            return fused(batch // 2, queries, slab, positives)
        return plain(queries, slab, positives)

    return jax.shard_map(
        per_device,
        mesh=mesh,
        in_specs=(P("batch", None), P(("label", "batch"), None), P("batch", "label")),
        out_specs=(P("batch", None), P(("label", "batch"), None)),
        check_vma=False,
    )
```
